32 devices in a mesh: seq: 8 (over z, x), exp: 4 (over y, core).
Axes of the slice: x: 2, y: 2, z: 4, core: 2. Of those that a mesh axis runs over, the one named last changes fastest.
Arguments:
- mixer_input: bfloat16 [512, 8192], P('seq', 'exp'), may hold values from -6 to 6
- gate_input: bfloat16 [512, 8192], P('seq', 'exp'), may hold values from -6 to 6
- conv_weight: bfloat16 [4, 8192], P(None, 'exp'), may hold values from -3 to 3
- conv_bias: float32 [8192], P('exp'), may hold values from -3 to 3
- rank_weight: bfloat16 [8192, 256], P('exp'), may hold values from -0.0625 to 0.0625
- state_weight: bfloat16 [8192, 32], P('exp'), may hold values from -0.03125 to 0.03125
- delta_weight: bfloat16 [256, 8192], P(None, 'exp'), may hold values from -0.375 to 0.375
- delta_bias: float32 [8192], P('exp'), may hold values from -1 to 1
- log_rates: float32 [16, 8192], P(None, 'exp'), may hold values from -10 to -1
- skip_gain: float32 [8192], P('exp'), may hold values from 0.5 to 1.5
- out_proj: bfloat16 [8192, 4096], P('exp', 'seq'), may hold values from -0.0625 to 0.0625
- residual: bfloat16 [512, 4096], P(('seq', 'exp')), may hold values from -3 to 3
- norm_gain: float32 [4096], replicated, may hold values from 0.5 to 1.5
- router: float32 [4096, 4], replicated, may hold values from -0.09375 to 0.09375
- w_gate: bfloat16 [4, 4096, 14336], P('exp', None, 'seq'), may hold values from -0.09375 to 0.09375
- w_up: bfloat16 [4, 4096, 14336], P('exp', None, 'seq'), may hold values from -0.09375 to 0.09375
- w_down: bfloat16 [4, 14336, 4096], P('exp', 'seq'), may hold values from -0.09375 to 0.09375
- routes: int32 [512, 2], P(('seq', 'exp')), may hold values from 0 to 3, all different within a row; in each aligned block of 16 rows (0 to 15, 16 to 31, ...) at most 16 rows name the same one
Outputs:
- layer_out: bfloat16 [512, 4096], P(('seq', 'exp'))
- expert_mix: float32 [512, 4096], P(('seq', 'exp'))
The draws below stay inside these ranges and needn't reach their ends.
Inputs may be any that keep to these rules, and one draw needn't show every extreme that they name: `routes`: each row names two different experts; among the 16 rows of one device no expert is named more than 16 times, a bound that some block reaches there on some device.
All inputs are finite; a program needn't handle non-finite values.
Results may differ from the reference program's by a relative error of at most 0.024.
Values may be sent and summed in bfloat16 or wider, within the bound.
A program may use at most 128 MiB of HBM per device.

```python
import math
import jax
import jax.numpy as jnp
import numpy as np
from jax import lax

D = 4096
INNER = 8192
STATE = 16
DT_RANK = 256
CONV = 4
FF = 14336
TOK_DEV = 16
SEQ_LEN = 512
EXPERTS = 4
CAP = 16
SLOTS = 512
N_SEQ = 8


def draw_log_rates(key, part):
    key_kind, key_slow, key_fast, key_extra = jax.random.split(key, 4)
    share = 0.5
    chain_level = -math.log(float(SEQ_LEN))
    slow_kind = jax.random.uniform(key_kind, (1, INNER), jnp.float32) < share
    slow_vals = chain_level + jax.random.uniform(key_slow, (STATE, INNER), jnp.float32, -1.2, 0.0)
    fast_vals = jax.random.uniform(key_fast, (STATE, INNER), jnp.float32, -3.5, -2.3)
    extra = jax.random.uniform(key_extra, (STATE, INNER), jnp.float32, 0.0, 0.7)
    return (jnp.where(slow_kind, slow_vals, fast_vals) + extra).astype(jnp.float32)


def shard_levels(rng, extent, cuts, smallest, largest):
    def one(dim, blocks):
        heights = jax.random.uniform(jax.random.fold_in(jax.random.fold_in(rng, 6), dim), (blocks,), jnp.float32, smallest / len(cuts), largest / len(cuts))
        return jnp.repeat(jnp.exp(heights), extent[dim] // blocks).reshape((-1,) + (1,) * (len(extent) - dim - 1))

    level = one(*cuts[0])
    for cut in cuts[1:]:
        level = level * one(*cut)
    return level


def deal_out(own_key, own, number, rows, number_of, top, reach, slope):
    order = jax.random.permutation(own_key, number_of)
    heavy_load, usual = portions_of(number_of, rows * top, reach, slope, True), portions_of(number_of, rows * top, reach, slope, False)
    places = jnp.arange(number_of)

    def named(tallies, rotation):
        used = int((tallies > 0).sum())
        fixed = max(1, used // 4)
        moved = fixed + (places - fixed + rotation * (used - fixed)) % max(1, number_of - fixed)
        return jnp.zeros((number_of,), jnp.int32).at[order[jnp.where(places < fixed, places, moved)]].set(jnp.asarray(tallies, jnp.int32))

    tallies = jnp.where(number % 4 == 0, named(heavy_load, number // 4), named(usual, number - number // 4 - 1))
    mixed = jax.random.permutation(jax.random.fold_in(own, 3), number_of)
    source_of, sink = mixed[0:number_of // 2 * 2:2], mixed[1:number_of // 2 * 2:2]
    slack = jnp.minimum(tallies[source_of] - 1, reach - tallies[sink]) // 2
    slack = jnp.where((source_of == order[0]) | (sink == order[0]) | (tallies[sink] == 0), 0, jnp.maximum(slack, 0))
    moved = jax.random.randint(jax.random.fold_in(own, 4), (number_of // 2,), 0, 1 << 20) % (slack + 1)
    tallies = tallies.at[source_of].add(-moved).at[sink].add(moved)
    items = jnp.searchsorted(jnp.cumsum(tallies), jnp.arange(rows * top), side="right").astype(jnp.int32)
    grid = items.reshape(top, rows).T
    grid = grid[jax.random.permutation(jax.random.fold_in(own, 1), rows)]
    rotation = jax.random.randint(jax.random.fold_in(own, 2), (rows, 1), 0, top)
    return jnp.take_along_axis(grid, (jnp.arange(top)[None, :] + rotation) % top, axis=1)


def portions_of(amount, total, reach, slope, full):
    portions = [(1 << 20) // math.isqrt(grade ** slope) + 1 for grade in range(1, amount + 1)]
    largest = reach if full else min(reach, max(-(-total // amount), total * portions[0] // sum(portions)))
    least = 1 if total - largest >= amount - 1 else 0
    holding, surplus = [largest] + [least] * (amount - 1), total - largest - least * (amount - 1)
    while surplus > 0:
        candidates = [i for i in range(1, amount) if holding[i] < largest] or [i for i in range(1, amount) if holding[i] < reach]
        mass, left = sum([portions[i] for i in candidates]), surplus
        for i in candidates:
            more = min(reach - holding[i], max(1, left * portions[i] // mass), surplus)
            holding[i] = holding[i] + more
            surplus = surplus - more
    return np.array(holding)


def noise(stream_key, shape, scale, reach, cuts=(), kind=jnp.bfloat16):
    entries = scale * jax.random.normal(stream_key, shape, jnp.float32)
    if cuts:
        entries = entries * shard_levels(stream_key, shape, cuts, -0.22, 0.18)
    return jnp.clip(entries, -reach, reach).astype(kind)


def setup_inputs(seed: int = 0) -> dict:
    key_of = jax.random.split(jax.random.key(seed), 19)
    mixer_input = noise(key_of[0], (SEQ_LEN, INNER), 1.0, 6.0, ((0, 8), (1, 4)))
    gate_input = noise(key_of[1], (SEQ_LEN, INNER), 1.0, 6.0, ((0, 8), (1, 4)))
    conv_weight = noise(key_of[2], (CONV, INNER), CONV ** -0.5, 3.0, ((1, 4),))
    conv_bias = noise(key_of[3], (INNER,), 0.5, 3.0, ((0, 4),), jnp.float32)
    rank_weight = noise(key_of[4], (INNER, DT_RANK), INNER ** -0.5, 0.0625, ((0, 4),))
    state_weight = noise(key_of[5], (INNER, 2 * STATE), (INNER * 4) ** -0.5, 0.03125, ((0, 4),))
    delta_weight = noise(key_of[6], (DT_RANK, INNER), DT_RANK ** -0.5, 0.375, ((1, 4),))
    delta_bias = jnp.clip(jax.random.uniform(key_of[7], (INNER,), jnp.float32, -1.0, 1.0) * shard_levels(key_of[7], (INNER,), ((0, 4),), -0.4, 0.0), -1.0, 1.0)
    log_rates = draw_log_rates(jax.random.fold_in(key_of[18], 71), 0)
    skip_gain = jnp.clip(0.5 + 1.0 * jax.random.uniform(key_of[9], (INNER,), jnp.float32) ** shard_levels(key_of[9], (INNER,), ((0, 4),), -0.2, 0.2), 0.5, 1.5)
    out_proj = noise(key_of[10], (INNER, D), INNER ** -0.5, 0.0625, ((0, 4), (1, 8)))
    residual = noise(key_of[11], (SEQ_LEN, D), 0.5, 3.0, ((0, 32),))
    norm_gain = jnp.clip(1.0 + 0.1 * jax.random.normal(key_of[12], (D,), jnp.float32), 0.5, 1.5)
    router = noise(key_of[13], (D, EXPERTS), D ** -0.5, 0.09375, (), jnp.float32)
    w_gate = noise(key_of[14], (EXPERTS, D, FF), D ** -0.5, 0.09375, ((0, 4), (2, 8)))
    w_up = noise(key_of[15], (EXPERTS, D, FF), D ** -0.5, 0.09375, ((0, 4), (2, 8)))
    w_down = noise(key_of[16], (EXPERTS, FF, D), (FF // 4) ** -0.5, 0.09375, ((0, 4), (1, 8)))
    routes_keys = jax.random.split(jax.random.fold_in(key_of[17], 1), SEQ_LEN // TOK_DEV)
    routes_turns = jax.random.permutation(jax.random.fold_in(key_of[17], 3), SEQ_LEN // TOK_DEV)
    routes = jax.vmap(lambda own, number: deal_out(jax.random.fold_in(key_of[17], 2), own, number, TOK_DEV, EXPERTS, 2, CAP, 2))(routes_keys, routes_turns).reshape((SEQ_LEN, 2))
    return dict(mixer_input=mixer_input, gate_input=gate_input, conv_weight=conv_weight, conv_bias=conv_bias, rank_weight=rank_weight, state_weight=state_weight, delta_weight=delta_weight, delta_bias=delta_bias, log_rates=log_rates, skip_gain=skip_gain, out_proj=out_proj, residual=residual, norm_gain=norm_gain, router=router, w_gate=w_gate, w_up=w_up, w_down=w_down, routes=routes)


def reference(mixer_input, gate_input, conv_weight, conv_bias, rank_weight, state_weight, delta_weight, delta_bias, log_rates, skip_gain, out_proj, residual, norm_gain, router, w_gate, w_up, w_down, routes):
    padded = jnp.concatenate([jnp.zeros((CONV - 1, INNER), jnp.bfloat16), mixer_input], axis=0)
    conv_sum = jnp.zeros((SEQ_LEN, INNER), jnp.float32) + conv_bias[None, :]
    for offset in range(CONV):
        conv_sum = conv_sum + conv_weight[offset].astype(jnp.float32)[None, :] * padded[offset:offset + SEQ_LEN].astype(jnp.float32)
    conv_act = jax.nn.silu(conv_sum).astype(jnp.bfloat16)
    delta_low = jnp.dot(conv_act, rank_weight, preferred_element_type=jnp.float32).astype(jnp.bfloat16)
    state_maps = jnp.dot(conv_act, state_weight, preferred_element_type=jnp.float32)
    input_map = state_maps[:, :STATE]
    output_map = state_maps[:, STATE:]
    delta = jax.nn.softplus(jnp.dot(delta_low, delta_weight, preferred_element_type=jnp.float32) + delta_bias[None, :])
    decay_rate = jnp.exp(log_rates)
    conv_float = conv_act.astype(jnp.float32)

    def advance(carried, inputs):
        delta_t, conv_t, input_t, output_t = inputs
        carried = jnp.exp(-delta_t[None, :] * decay_rate) * carried + (delta_t * conv_t)[None, :] * input_t[:, None]
        return (carried, lax.optimization_barrier(jnp.sum(output_t[:, None] * carried, axis=0)))
    final_state, scan_out = lax.scan(advance, jnp.zeros((STATE, INNER), jnp.float32), (delta, conv_float, input_map, output_map))
    scan_out = scan_out + skip_gain[None, :] * conv_float
    gated = (scan_out * jax.nn.silu(gate_input.astype(jnp.float32))).astype(jnp.bfloat16)
    mamba_out = jnp.dot(gated, out_proj, preferred_element_type=jnp.float32)
    hidden = residual.astype(jnp.float32) + mamba_out
    mean_square = lax.optimization_barrier(jnp.mean(hidden * hidden, axis=1, keepdims=True))
    normed = (hidden * lax.rsqrt(mean_square + 1e-05) * norm_gain[None, :]).astype(jnp.bfloat16)
    logits = jnp.dot(normed.astype(jnp.float32), router, precision=lax.Precision.HIGHEST)
    chosen = jnp.take_along_axis(logits, routes, axis=1)
    route_weights = jax.nn.sigmoid(chosen - chosen[:, ::-1]).reshape(-1)
    flat_ids = routes.reshape(-1)
    route_pos = jnp.arange(2 * SEQ_LEN, dtype=jnp.int32)
    group_size = FF // N_SEQ

    def per_expert(total_out, expert):
        sort_keys = jnp.where(flat_ids == expert, route_pos, 2 * SEQ_LEN).astype(jnp.int32)
        picked = jnp.sort(sort_keys)[:SLOTS]
        is_valid = picked < 2 * SEQ_LEN
        safe_pos = jnp.minimum(picked, 2 * SEQ_LEN - 1).astype(jnp.int32)
        token_rows = (safe_pos // 2).astype(jnp.int32)
        rows_in = jnp.take(normed, token_rows, axis=0)
        gate_part = jnp.dot(rows_in, w_gate[expert], preferred_element_type=jnp.float32)
        up_part = jnp.dot(rows_in, w_up[expert], preferred_element_type=jnp.float32)
        activated = (jax.nn.silu(gate_part) * up_part).astype(jnp.bfloat16)
        act_groups = activated.reshape(SLOTS, N_SEQ, group_size).transpose(1, 0, 2)
        down_groups = w_down[expert].reshape(N_SEQ, group_size, D)

        def add_group(running, group_pair):
            act_group, down_group = group_pair
            group_term = jnp.dot(act_group, down_group, preferred_element_type=jnp.float32).astype(jnp.bfloat16)
            group_term = lax.optimization_barrier(group_term)
            return (running + group_term.astype(jnp.float32), None)
        expert_out, unused = lax.scan(add_group, jnp.zeros((SLOTS, D), jnp.float32), (act_groups, down_groups))
        weight_col = jnp.where(is_valid, jnp.take(route_weights, safe_pos), 0.0)
        total_out = total_out.at[token_rows].add(weight_col[:, None] * expert_out)
        return (total_out, None)
    moe_sum, unused = lax.scan(per_expert, jnp.zeros((SEQ_LEN, D), jnp.float32), jnp.arange(EXPERTS, dtype=jnp.int32))
    return ((hidden + moe_sum).astype(jnp.bfloat16), moe_sum)
```

```python
import functools

import jax
import jax.numpy as jnp
from jax import lax
from jax.experimental import pallas as pl
from jax.experimental.pallas import tpu as pltpu
from jax.sharding import PartitionSpec as P

MESH = pl.DeviceIdType.MESH
BF16 = jnp.bfloat16
F32 = jnp.float32
VMEM_BYTES = 58 * 1024 * 1024
ORDER = "zxyc"


def axis_sizes(seq, exp):
    x = 1
    while 4 * x * x <= seq and seq % (2 * x) == 0:
        x *= 2
    c = 2 if exp % 2 == 0 else 1
    return {"z": seq // x, "x": x, "y": exp // c, "c": c}


def own_place(size):
    seq, exp = lax.axis_index("seq"), lax.axis_index("exp")
    return {"z": seq // size["x"], "x": seq % size["x"], "y": exp // size["c"], "c": exp % size["c"]}


def device_at(place, size):
    return (place["z"] * size["x"] + place["x"], place["y"] * size["c"] + place["c"])


def moved(place, size, axis, distance):
    return {**place, axis: (place[axis] + distance) % size[axis]}


def greet(size, axes):
    me = own_place(size)
    barrier = pltpu.get_barrier_semaphore()
    count = 0
    for axis in axes:
        for d in range(1, size[axis]):
            pl.semaphore_signal(
                barrier, inc=1, device_id=device_at(moved(me, size, axis, d), size), device_id_type=MESH
            )
            count += 1
    pl.semaphore_wait(barrier, count)


def held_after(size, axes):
    held = [()]
    for axis in axes:
        held = [h + (d,) for h in held for d in range(size[axis])]
    return held


def gather_kernel(size, flows, x_ref, out_ref, send_sem, recv_sem, own_sem):
    me = own_place(size)
    axes = [a for a in ORDER if a in flows[0][0]]
    greet(size, axes)

    def slot(offsets, path):
        place = dict(me)
        for axis, d in zip(path, offsets):
            place[axis] = (me[axis] + d) % size[axis]
        return tuple(place[a] for a in axes)

    own = pltpu.make_async_copy(x_ref, out_ref.at[slot((), ())], own_sem)
    own.start()
    sends, arrived, number = [], set(), {}
    for f, (path, _, _) in enumerate(flows):
        for offsets in held_after(size, path):
            number[(f, offsets)] = len(number)

    def window(ref, lo, hi):
        return ref.at[:, lo:hi]

    def arrive(f, offsets):
        path, lo, hi = flows[f]
        full = offsets + (0,) * (len(path) - len(offsets))
        if any(full) and (f, full) not in arrived:
            arrived.add((f, full))
            landing = window(out_ref.at[slot(full, path)], lo, hi)
            pltpu.make_async_copy(landing, landing, recv_sem.at[number[(f, full)]]).wait()

    for stage in range(len(flows[0][0])):
        for offsets in held_after(size, flows[0][0][:stage]):
            pass
        lists = [held_after(size, path[:stage]) for path, _, _ in flows]
        for k in range(max(len(held) for held in lists)):
            for f, (path, lo, hi) in enumerate(flows):
                if k >= len(lists[f]):
                    continue
                offsets = lists[f][k]
                arrive(f, offsets)
                axis = path[stage]
                for d in range(1, size[axis]):
                    here = slot(offsets, path)
                    source = x_ref if not any(offsets) else out_ref.at[here]
                    lands = offsets + ((size[axis] - d),) + (0,) * (len(path) - stage - 1)
                    copy = pltpu.make_async_remote_copy(
                        src_ref=window(source, lo, hi),
                        dst_ref=window(out_ref.at[here], lo, hi),
                        send_sem=send_sem.at[len(sends)],
                        recv_sem=recv_sem.at[number[(f, lands)]],
                        device_id=device_at(moved(me, size, axis, d), size),
                        device_id_type=MESH,
                    )
                    copy.start()
                    sends.append(copy)
    for f, (path, _, _) in enumerate(flows):
        for offsets in held_after(size, path):
            arrive(f, offsets)
    for copy in sends:
        copy.wait_send()
    own.wait()


def gather(block, size, paths, splits, collective_id):
    axes = [a for a in ORDER if a in paths[0]]
    edges = (0,) + tuple(splits) + (block.shape[1],)
    flows = [(tuple(p), lo, hi) for p, lo, hi in zip(paths, edges[:-1], edges[1:])]
    slots = len(flows)
    for a in axes:
        slots *= size[a]
    return pl.pallas_call(
        functools.partial(gather_kernel, size, flows),
        out_shape=jax.ShapeDtypeStruct(tuple(size[a] for a in axes) + block.shape, block.dtype),
        in_specs=[pl.BlockSpec(memory_space=pl.ANY)],
        out_specs=pl.BlockSpec(memory_space=pl.ANY),
        scratch_shapes=[
            pltpu.SemaphoreType.DMA((slots,)),
            pltpu.SemaphoreType.DMA((slots,)),
            pltpu.SemaphoreType.DMA,
        ],
        compiler_params=pltpu.CompilerParams(
            collective_id=collective_id, has_side_effects=True, vmem_limit_bytes=VMEM_BYTES
        ),
        name="gather_" + "".join(axes),
    )(block)


def channels_kernel(size, part_ref, out_ref, landed, summed, spread, send_sem, recv_sem, send2, recv2):
    seq, exp = size["z"] * size["x"], size["y"] * size["c"]
    s, e = lax.axis_index("seq"), lax.axis_index("exp")
    barrier = pltpu.get_barrier_semaphore()
    for d in range(1, exp):
        pl.semaphore_signal(barrier, inc=1, device_id=(s, (e + d) % exp), device_id_type=MESH)
    for d in range(1, seq):
        pl.semaphore_signal(barrier, inc=1, device_id=((s + d) % seq, e), device_id_type=MESH)
    pl.semaphore_wait(barrier, exp + seq - 2)
    copies = []
    for d in range(1, exp):
        to = (e + d) % exp
        copy = pltpu.make_async_remote_copy(
            src_ref=part_ref.at[to],
            dst_ref=landed.at[exp - d - 1],
            send_sem=send_sem.at[d - 1],
            recv_sem=recv_sem.at[exp - d - 1],
            device_id=(s, to),
            device_id_type=MESH,
        )
        copy.start()
        copies.append(copy)
    for copy in copies:
        copy.wait()

    def add(k, carry):
        total = part_ref[e, k].astype(F32)
        for d in range(exp - 1):
            total = total + landed[d, k].astype(F32)
        summed[k] = total.astype(BF16)
        return carry

    lax.fori_loop(0, seq, add, 0)
    copies = []
    for d in range(1, seq):
        to = (s + d) % seq
        copy = pltpu.make_async_remote_copy(
            src_ref=summed.at[to],
            dst_ref=spread.at[s],
            send_sem=send2.at[d - 1],
            recv_sem=recv2.at[seq - d - 1],
            device_id=(to, e),
            device_id_type=MESH,
        )
        copy.start()
        copies.append(copy)
    for copy in copies:
        copy.wait_send()
    for d in range(1, seq):
        block = spread.at[(s + d) % seq]
        pltpu.make_async_copy(block, block, recv2.at[d - 1]).wait()
    spread[s] = summed[s]
    width = spread.shape[2]
    for k in range(seq):
        out_ref[:, k * width : (k + 1) * width] = spread[k].astype(F32)


def sum_channels(part, size, collective_id):
    exp, seq, rows, width = part.shape
    return pl.pallas_call(
        functools.partial(channels_kernel, size),
        out_shape=jax.ShapeDtypeStruct((rows, seq * width), F32),
        in_specs=[pl.BlockSpec(memory_space=pltpu.VMEM)],
        out_specs=pl.BlockSpec(memory_space=pltpu.VMEM),
        scratch_shapes=[
            pltpu.VMEM((exp - 1, seq, rows, width), BF16),
            pltpu.VMEM((seq, rows, width), BF16),
            pltpu.VMEM((seq, rows, width), BF16),
            pltpu.SemaphoreType.DMA((exp - 1,)),
            pltpu.SemaphoreType.DMA((exp - 1,)),
            pltpu.SemaphoreType.DMA((seq - 1,)),
            pltpu.SemaphoreType.DMA((seq - 1,)),
        ],
        compiler_params=pltpu.CompilerParams(
            collective_id=collective_id, has_side_effects=True, vmem_limit_bytes=VMEM_BYTES
        ),
        name="sum_channels",
    )(part)


def experts_kernel(size, part_ref, out_ref, *scratch):
    me = own_place(size)
    greet(size, "zxyc")
    half = part_ref.shape[-1] // 2
    rows = part_ref.shape[-2]
    from_core, first_a, first_b, land_a, land_b, second_a, second_b, land2_a, land2_b = scratch[:9]
    third_a, third_b, land3_a, land3_b, core_sems, sems = scratch[9:]
    cores = size["c"]
    pending = []
    if cores == 2:
        copy = pltpu.make_async_remote_copy(
            src_ref=part_ref.at[:, :, :, 1 - me["c"]],
            dst_ref=from_core,
            send_sem=core_sems.at[0],
            recv_sem=core_sems.at[1],
            device_id=device_at(moved(me, size, "c", 1), size),
            device_id_type=MESH,
        )
        copy.start()
        copy.wait()

    def first(i, carry):
        z, x, y = i // (size["x"] * size["y"]), (i // size["y"]) % size["x"], i % size["y"]
        for lo, target in ((0, first_a.at[y, x, z]), (half, first_b.at[x, y, z])):
            total = part_ref[z, x, y, me["c"], :, lo : lo + half].astype(F32)
            if cores == 2:
                total = total + from_core[z, x, y, :, lo : lo + half].astype(F32)
            target[...] = total.astype(BF16)
        return carry

    lax.fori_loop(0, size["x"] * size["y"] * size["z"], first, 0)
    used = [0]

    def exchange(axis, source, landing):
        copies = []
        for d in range(1, size[axis]):
            to = moved(me, size, axis, d)
            copy = pltpu.make_async_remote_copy(
                src_ref=source.at[to[axis]],
                dst_ref=landing.at[size[axis] - d - 1],
                send_sem=sems.at[used[0] + d - 1],
                recv_sem=sems.at[used[0] + 2 * (size[axis] - 1) - d],
                device_id=device_at(to, size),
                device_id_type=MESH,
            )
            copy.start()
            copies.append(copy)
        used[0] += 2 * (size[axis] - 1)
        return copies

    def add(axis, source, landing, target, inner):
        def one(i, carry):
            place = (i // inner, i % inner) if len(target.shape) == 4 else (i,)
            total = source[(me[axis],) + place].astype(F32)
            for d in range(size[axis] - 1):
                total = total + landing[(d,) + place].astype(F32)
            target[place] = total.astype(BF16)
            return carry

        count = 1
        for extent in target.shape[:-2]:
            count *= extent
        lax.fori_loop(0, count, one, 0)

    for copy_a, copy_b in [(exchange("y", first_a, land_a), exchange("x", first_b, land_b))]:
        for copy in copy_a:
            copy.wait()
        add("y", first_a, land_a, second_a, size["z"])
        copy2_a = exchange("x", second_a, land2_a)
        for copy in copy_b:
            copy.wait()
        add("x", first_b, land_b, second_b, size["z"])
        copy2_b = exchange("y", second_b, land2_b)
        for copy in copy2_a:
            copy.wait()
        add("x", second_a, land2_a, third_a, 1)
        copy3_a = exchange("z", third_a, land3_a)
        for copy in copy2_b:
            copy.wait()
        add("y", second_b, land2_b, third_b, 1)
        copy3_b = exchange("z", third_b, land3_b)
        for lo, third, landing, copies in ((0, third_a, land3_a, copy3_a), (half, third_b, land3_b, copy3_b)):
            for copy in copies:
                copy.wait()
            total = third[me["z"]].astype(F32)
            for d in range(size["z"] - 1):
                total = total + landing[d].astype(F32)
            out_ref[:, lo : lo + half] = total


def sum_experts(part, size, collective_id):
    rows, width = part.shape[-2:]
    half = width // 2
    x, y, z = size["x"], size["y"], size["z"]

    def buffer(*lead):
        return pltpu.VMEM(lead + (rows, half), BF16)

    return pl.pallas_call(
        functools.partial(experts_kernel, size),
        out_shape=jax.ShapeDtypeStruct((rows, width), F32),
        in_specs=[pl.BlockSpec(memory_space=pltpu.VMEM)],
        out_specs=pl.BlockSpec(memory_space=pltpu.VMEM),
        scratch_shapes=[
            pltpu.VMEM((z, x, y, rows, width), BF16),
            buffer(y, x, z),
            buffer(x, y, z),
            buffer(y - 1, x, z),
            buffer(x - 1, y, z),
            buffer(x, z),
            buffer(y, z),
            buffer(x - 1, z),
            buffer(y - 1, z),
            buffer(z),
            buffer(z),
            buffer(z - 1),
            buffer(z - 1),
            pltpu.SemaphoreType.DMA((2,)),
            pltpu.SemaphoreType.DMA((4 * (x + y + z - 3),)),
        ],
        compiler_params=pltpu.CompilerParams(
            collective_id=collective_id, has_side_effects=True, vmem_limit_bytes=VMEM_BYTES
        ),
        name="sum_experts",
    )(part)


def lane_tiles(column, lanes):
    return jnp.concatenate([column] * (lanes // column.shape[1]), axis=1)


def end_kernel(delta_ref, drive_ref, input_ref, rate_ref, end_ref):
    rate = -jnp.exp(rate_ref[...])
    lanes = rate.shape[1]

    def step(t, state):
        decay = jnp.exp(delta_ref[pl.ds(t, 1), :] * rate)
        return decay * state + drive_ref[pl.ds(t, 1), :] * lane_tiles(input_ref[t], lanes)

    end_ref[...] = lax.fori_loop(0, delta_ref.shape[0], step, jnp.zeros_like(rate), unroll=8)


def scan_kernel(
    delta_ref, drive_ref, input_ref, output_ref, rate_ref, start_ref, conv_ref, gate_ref, skip_ref, out_ref, y_ref
):
    rate = -jnp.exp(rate_ref[...])
    lanes = rate.shape[1]

    def step(t, state):
        decay = jnp.exp(delta_ref[pl.ds(t, 1), :] * rate)
        state = decay * state + drive_ref[pl.ds(t, 1), :] * lane_tiles(input_ref[t], lanes)
        y_ref[pl.ds(t, 1), :] = jnp.sum(state * lane_tiles(output_ref[t], lanes), axis=0, keepdims=True)
        return state

    lax.fori_loop(0, delta_ref.shape[0], step, start_ref[...], unroll=8)
    scan_out = y_ref[...] + skip_ref[...] * conv_ref[...].astype(F32)
    gate = gate_ref[...].astype(F32)
    out_ref[...] = (scan_out * (gate * jax.nn.sigmoid(gate))).astype(BF16)


def scan_specs(rows, states, lanes):
    wide = pl.BlockSpec((rows, lanes), lambda i: (0, i))
    maps = pl.BlockSpec((rows, states, 128), lambda i: (0, 0, 0))
    state = pl.BlockSpec((states, lanes), lambda i: (0, i))
    return wide, maps, state, pl.BlockSpec((1, lanes), lambda i: (0, i))


def body(
    mixer_input,
    gate_input,
    conv_weight,
    conv_bias,
    rank_weight,
    state_weight,
    delta_weight,
    delta_bias,
    log_rates,
    skip_gain,
    out_proj,
    residual,
    norm_gain,
    router,
    w_gate,
    w_up,
    w_down,
    routes,
):
    seq, exp = lax.axis_size("seq"), lax.axis_size("exp")
    size = axis_sizes(seq, exp)
    taps = conv_weight.shape[0]
    block_rows, width = mixer_input.shape
    route = [(i - 1, i) for i in range(1, seq)]
    rim_rows = lax.ppermute(mixer_input[block_rows - (taps - 1) :], "seq", route)
    padded = jnp.concatenate([rim_rows, mixer_input], axis=0)
    conv_sum = jnp.zeros(mixer_input.shape, F32) + conv_bias[None, :]
    for offset in range(taps):
        conv_sum = conv_sum + conv_weight[offset].astype(F32)[None, :] * padded[
            offset : offset + block_rows
        ].astype(F32)
    conv_act = jax.nn.silu(conv_sum).astype(BF16)
    rank, states = rank_weight.shape[1], log_rates.shape[0]
    narrow = -(-(rank + 2 * states) // 128) * 128
    low_weight = jnp.concatenate(
        [rank_weight, state_weight, jnp.zeros((width, narrow - rank - 2 * states), BF16)], axis=1
    )
    low_part = jnp.dot(conv_act, low_weight, preferred_element_type=F32)
    low = jnp.sum(gather(low_part, size, ("yc",), (), 1), axis=(0, 1))
    delta_low = low[:, :rank].astype(BF16)
    input_map = low[:, rank : rank + states]
    output_map = low[:, rank + states : rank + 2 * states]
    delta = jax.nn.softplus(
        jnp.dot(delta_low, delta_weight, preferred_element_type=F32) + delta_bias[None, :]
    )
    drive = delta * conv_act.astype(F32)
    total_dt = jnp.sum(delta, axis=0)
    input_wide = jnp.broadcast_to(input_map[:, :, None], (block_rows, states, 128))
    output_wide = jnp.broadcast_to(output_map[:, :, None], (block_rows, states, 128))

    lanes = 512 if width % 512 == 0 else 128
    wide, maps, state, line = scan_specs(block_rows, states, lanes)
    last = pl.pallas_call(
        end_kernel,
        grid=(width // lanes,),
        out_shape=jax.ShapeDtypeStruct((states, width), F32),
        in_specs=[wide, wide, maps, state],
        out_specs=state,
        name="block_end",
    )(delta, drive, input_wide, log_rates)
    passing = jnp.concatenate([last, total_dt.reshape(states, width // states)], axis=1).astype(BF16)
    passed = gather(passing, size, ("zx",), (), 2).reshape((seq,) + passing.shape)
    index = lax.axis_index("seq")
    rate = jnp.exp(log_rates)
    start_state = jnp.zeros((states, width), F32)
    for k in range(seq - 1):
        gone = passed[k, :, width:].reshape(1, width).astype(F32)
        following = jnp.exp(-gone * rate) * start_state + passed[k, :, :width].astype(F32)
        start_state = jnp.where(k < index, following, start_state)
    gated = pl.pallas_call(
        scan_kernel,
        grid=(width // lanes,),
        out_shape=jax.ShapeDtypeStruct((block_rows, width), BF16),
        in_specs=[wide, wide, maps, maps, state, state, wide, wide, line],
        out_specs=wide,
        scratch_shapes=[pltpu.VMEM((block_rows, lanes), F32)],
        name="scan",
    )(delta, drive, input_wide, output_wide, log_rates, start_state, conv_act, gate_input, skip_gain[None, :])

    tok_dev, features = residual.shape
    everyone = gather(gated, size, ("zx",), (), 3).reshape(seq * block_rows, width)
    part = jnp.dot(everyone, out_proj, preferred_element_type=F32).astype(BF16)
    part = part.reshape(seq, exp, tok_dev, part.shape[1]).transpose(1, 0, 2, 3)
    hidden = residual.astype(F32) + sum_channels(part, size, 4)
    mean_square = jnp.mean(hidden * hidden, axis=1, keepdims=True)
    normed = (hidden * lax.rsqrt(mean_square + 1e-05) * norm_gain[None, :]).astype(BF16)
    logits = jnp.dot(normed.astype(F32), router, precision=lax.Precision.HIGHEST)
    experts = router.shape[1]
    expert_ids = jnp.arange(experts, dtype=jnp.int32)
    matches = (routes[:, :, None] == expert_ids[None, None, :]).astype(F32)
    chosen = jnp.sum(matches * logits[:, None, :], axis=2)
    route_weights = jax.nn.sigmoid(chosen - chosen[:, ::-1])
    shares = jnp.sum(matches * route_weights[:, :, None], axis=1)
    shares = jnp.pad(shares, ((0, 0), (0, 128 - experts))).astype(BF16)
    rows = gather(
        jnp.concatenate([normed, shares], axis=1), size, ("zxyc", "zyxc"), (features // 2,), 5
    )
    rows = rows.reshape(seq * exp * tok_dev, features + 128)
    own_share = jnp.sum(
        jnp.where(
            jnp.arange(128)[None, :] == lax.axis_index("exp"), rows[:, features:].astype(F32), 0.0
        ),
        axis=1,
        keepdims=True,
    )
    rows = rows[:, :features]
    gate_part = jnp.dot(rows, w_gate[0], preferred_element_type=F32)
    up_part = jnp.dot(rows, w_up[0], preferred_element_type=F32)
    activated = (jax.nn.silu(gate_part) * up_part).astype(BF16)
    part = (jnp.dot(activated, w_down[0], preferred_element_type=F32) * own_share).astype(BF16)
    part = part.reshape(size["z"], size["x"], size["y"], size["c"], tok_dev, features)
    moe_sum = sum_experts(part, size, 6)
    return ((hidden + moe_sum).astype(BF16), moe_sum)


def solution(mesh):
    in_specs = (
        P("seq", "exp"),
        P("seq", "exp"),
        P(None, "exp"),
        P("exp"),
        P("exp", None),
        P("exp", None),
        P(None, "exp"),
        P("exp"),
        P(None, "exp"),
        P("exp"),
        P("exp", "seq"),
        P(("seq", "exp"), None),
        P(),
        P(),
        P("exp", None, "seq"),
        P("exp", None, "seq"),
        P("exp", "seq", None),
        P(("seq", "exp"), None),
    )
    out_specs = (P(("seq", "exp"), None), P(("seq", "exp"), None))
    return jax.shard_map(body, mesh=mesh, in_specs=in_specs, out_specs=out_specs, check_vma=False)
```

```python
import functools

import jax
import jax.numpy as jnp
from jax import lax
from jax.experimental import pallas as pl
from jax.experimental.pallas import tpu as pltpu
from jax.sharding import PartitionSpec as P

MESH = pl.DeviceIdType.MESH
BF16 = jnp.bfloat16
F32 = jnp.float32
VMEM_BYTES = 58 * 1024 * 1024
ORDER = "zxyc"


def axis_sizes(seq, exp):
    x = 1
    while 4 * x * x <= seq and seq % (2 * x) == 0:
        x *= 2
    c = 2 if exp % 2 == 0 else 1
    return {"z": seq // x, "x": x, "y": exp // c, "c": c}


def own_place(size):
    seq, exp = lax.axis_index("seq"), lax.axis_index("exp")
    return {"z": seq // size["x"], "x": seq % size["x"], "y": exp // size["c"], "c": exp % size["c"]}


def device_at(place, size):
    return (place["z"] * size["x"] + place["x"], place["y"] * size["c"] + place["c"])


def moved(place, size, axis, distance):
    return {**place, axis: (place[axis] + distance) % size[axis]}


def greet(size, axes):
    me = own_place(size)
    barrier = pltpu.get_barrier_semaphore()
    count = 0
    for axis in axes:
        for d in range(1, size[axis]):
            pl.semaphore_signal(
                barrier, inc=1, device_id=device_at(moved(me, size, axis, d), size), device_id_type=MESH
            )
            count += 1
    pl.semaphore_wait(barrier, count)


def held_after(size, axes):
    held = [()]
    for axis in axes:
        held = [h + (d,) for h in held for d in range(size[axis])]
    return held


def gather_kernel(size, flows, x_ref, out_ref, send_sem, recv_sem, own_sem):
    me = own_place(size)
    axes = [a for a in ORDER if a in flows[0][0]]
    greet(size, axes)

    def slot(offsets, path):
        place = dict(me)
        for axis, d in zip(path, offsets):
            place[axis] = (me[axis] + d) % size[axis]
        return tuple(place[a] for a in axes)

    own = pltpu.make_async_copy(x_ref, out_ref.at[slot((), ())], own_sem)
    own.start()
    sends, arrived, number = [], set(), {}
    for f, (path, _, _) in enumerate(flows):
        for offsets in held_after(size, path):
            number[(f, offsets)] = len(number)

    def window(ref, lo, hi):
        return ref.at[:, lo:hi]

    def arrive(f, offsets):
        path, lo, hi = flows[f]
        full = offsets + (0,) * (len(path) - len(offsets))
        if any(full) and (f, full) not in arrived:
            arrived.add((f, full))
            landing = window(out_ref.at[slot(full, path)], lo, hi)
            pltpu.make_async_copy(landing, landing, recv_sem.at[number[(f, full)]]).wait()

    def forward(f, offsets, stage):
        path, lo, hi = flows[f]
        here = slot(offsets, path)
        axis = path[stage]
        source = x_ref if not any(offsets) else out_ref.at[here]
        for d in range(1, size[axis]):
            lands = offsets[:stage] + (size[axis] - d,) + (0,) * (len(path) - stage - 1)
            copy = pltpu.make_async_remote_copy(
                src_ref=window(source, lo, hi),
                dst_ref=window(out_ref.at[here], lo, hi),
                send_sem=send_sem.at[len(sends)],
                recv_sem=recv_sem.at[number[(f, lands)]],
                device_id=device_at(moved(me, size, axis, d), size),
                device_id_type=MESH,
            )
            copy.start()
            sends.append(copy)

    stages = len(flows[0][0])
    for stage in range(stages):
        for f, (path, _, _) in enumerate(flows):
            forward(f, (0,) * stages, stage)
    alike = all(path == flows[0][0] for path, _, _ in flows)
    for came in range(stages):
        work = []
        for f, (path, _, _) in enumerate(flows):
            held = [h for h in held_after(size, path[: came + 1]) if h[came]]
            work += [(f if alike else k, f, h + (0,) * (stages - came - 1)) for k, h in enumerate(held)]
        for _, f, offsets in sorted(work, key=lambda item: item[0]):
            arrive(f, offsets)
            for stage in range(came + 1, stages):
                forward(f, offsets, stage)
    for f, (path, _, _) in enumerate(flows):
        for offsets in held_after(size, path):
            arrive(f, offsets)
    for copy in sends:
        copy.wait_send()
    own.wait()


def gather(block, size, paths, splits, collective_id):
    axes = [a for a in ORDER if a in paths[0]]
    edges = (0,) + tuple(splits) + (block.shape[1],)
    flows = [(tuple(p), lo, hi) for p, lo, hi in zip(paths, edges[:-1], edges[1:])]
    slots = len(flows)
    for a in axes:
        slots *= size[a]
    return pl.pallas_call(
        functools.partial(gather_kernel, size, flows),
        out_shape=jax.ShapeDtypeStruct(tuple(size[a] for a in axes) + block.shape, block.dtype),
        in_specs=[pl.BlockSpec(memory_space=pl.ANY)],
        out_specs=pl.BlockSpec(memory_space=pl.ANY),
        scratch_shapes=[
            pltpu.SemaphoreType.DMA((slots,)),
            pltpu.SemaphoreType.DMA((slots,)),
            pltpu.SemaphoreType.DMA,
        ],
        compiler_params=pltpu.CompilerParams(
            collective_id=collective_id, has_side_effects=True, vmem_limit_bytes=VMEM_BYTES
        ),
        name="gather_" + "".join(axes),
    )(block)


def channels_kernel(size, part_ref, out_ref, landed, summed, spread, send_sem, recv_sem, send2, recv2):
    seq, exp = size["z"] * size["x"], size["y"] * size["c"]
    s, e = lax.axis_index("seq"), lax.axis_index("exp")
    barrier = pltpu.get_barrier_semaphore()
    for d in range(1, exp):
        pl.semaphore_signal(barrier, inc=1, device_id=(s, (e + d) % exp), device_id_type=MESH)
    for d in range(1, seq):
        pl.semaphore_signal(barrier, inc=1, device_id=((s + d) % seq, e), device_id_type=MESH)
    pl.semaphore_wait(barrier, exp + seq - 2)
    copies = []
    for d in range(1, exp):
        to = (e + d) % exp
        copy = pltpu.make_async_remote_copy(
            src_ref=part_ref.at[to],
            dst_ref=landed.at[exp - d - 1],
            send_sem=send_sem.at[d - 1],
            recv_sem=recv_sem.at[exp - d - 1],
            device_id=(s, to),
            device_id_type=MESH,
        )
        copy.start()
        copies.append(copy)
    for copy in copies:
        copy.wait()

    def add(k, carry):
        total = part_ref[e, k].astype(F32)
        for d in range(exp - 1):
            total = total + landed[d, k].astype(F32)
        summed[k] = total.astype(BF16)
        return carry

    lax.fori_loop(0, seq, add, 0)
    copies = []
    for d in range(1, seq):
        to = (s + d) % seq
        copy = pltpu.make_async_remote_copy(
            src_ref=summed.at[to],
            dst_ref=spread.at[s],
            send_sem=send2.at[d - 1],
            recv_sem=recv2.at[seq - d - 1],
            device_id=(to, e),
            device_id_type=MESH,
        )
        copy.start()
        copies.append(copy)
    for copy in copies:
        copy.wait_send()
    for d in range(1, seq):
        block = spread.at[(s + d) % seq]
        pltpu.make_async_copy(block, block, recv2.at[d - 1]).wait()
    spread[s] = summed[s]
    width = spread.shape[2]
    for k in range(seq):
        out_ref[:, k * width : (k + 1) * width] = spread[k].astype(F32)


def sum_channels(part, size, collective_id):
    exp, seq, rows, width = part.shape
    return pl.pallas_call(
        functools.partial(channels_kernel, size),
        out_shape=jax.ShapeDtypeStruct((rows, seq * width), F32),
        in_specs=[pl.BlockSpec(memory_space=pltpu.VMEM)],
        out_specs=pl.BlockSpec(memory_space=pltpu.VMEM),
        scratch_shapes=[
            pltpu.VMEM((exp - 1, seq, rows, width), BF16),
            pltpu.VMEM((seq, rows, width), BF16),
            pltpu.VMEM((seq, rows, width), BF16),
            pltpu.SemaphoreType.DMA((exp - 1,)),
            pltpu.SemaphoreType.DMA((exp - 1,)),
            pltpu.SemaphoreType.DMA((seq - 1,)),
            pltpu.SemaphoreType.DMA((seq - 1,)),
        ],
        compiler_params=pltpu.CompilerParams(
            collective_id=collective_id, has_side_effects=True, vmem_limit_bytes=VMEM_BYTES
        ),
        name="sum_channels",
    )(part)


def experts_kernel(size, part_ref, out_ref, *scratch):
    me = own_place(size)
    greet(size, "zxyc")
    chunks = part_ref.shape[0]
    width = part_ref.shape[-1]
    half = width // 2
    from_core, core_send, core_recv, sems = scratch[:4]
    flows = (("yxz", scratch[4:9], 0), ("xyz", scratch[9:14], half))
    hops = sum(size[a] - 1 for a in "xyz")

    def exchange(axis, chunk, flow, before, source, landing):
        copies = []
        base = (chunk * 2 + flow) * hops + before
        for d in range(1, size[axis]):
            to = moved(me, size, axis, d)
            copy = pltpu.make_async_remote_copy(
                src_ref=source.at[chunk, to[axis]],
                dst_ref=landing.at[chunk, size[axis] - d - 1],
                send_sem=sems.at[0, base + d - 1],
                recv_sem=sems.at[1, base + size[axis] - d - 1],
                device_id=device_at(to, size),
                device_id_type=MESH,
            )
            copy.start()
            copies.append(copy)
        return copies

    core_copies = []
    if size["c"] == 2:
        for chunk in range(chunks):
            copy = pltpu.make_async_remote_copy(
                src_ref=part_ref.at[chunk, :, :, :, 1 - me["c"]],
                dst_ref=from_core.at[chunk],
                send_sem=core_send.at[chunk],
                recv_sem=core_recv.at[chunk],
                device_id=device_at(moved(me, size, "c", 1), size),
                device_id_type=MESH,
            )
            copy.start()
            core_copies.append(copy)
    flight = {}

    def begin(chunk):
        if core_copies:
            core_copies[chunk].wait()

        def first(i, carry):
            z, x, y = i // (size["x"] * size["y"]), (i // size["y"]) % size["x"], i % size["y"]
            total = part_ref[chunk, z, x, y, me["c"]].astype(F32)
            if core_copies:
                total = total + from_core[chunk, z, x, y].astype(F32)
            total = total.astype(BF16)
            flows[0][1][0][chunk, y, x, z] = total[:, :half]
            flows[1][1][0][chunk, x, y, z] = total[:, half:]
            return carry

        lax.fori_loop(0, size["x"] * size["y"] * size["z"], first, 0)
        for f, (axes, buffers, _) in enumerate(flows):
            flight[(chunk, f)] = exchange(axes[0], chunk, f, 0, buffers[0], buffers[1])

    def middle(chunk):
        for f, (axes, buffers, _) in enumerate(flows):
            for copy in flight[(chunk, f)]:
                copy.wait()
            source, landing, second, landing2, _ = buffers
            inner = size["z"]

            def one(i, carry, axis=axes[0], source=source, landing=landing, second=second):
                total = source[chunk, me[axis], i // inner, i % inner].astype(F32)
                for d in range(size[axis] - 1):
                    total = total + landing[chunk, d, i // inner, i % inner].astype(F32)
                second[chunk, i // inner, i % inner] = total.astype(BF16)
                return carry

            lax.fori_loop(0, size[axes[1]] * inner, one, 0)
            flight[(chunk, f)] = exchange(axes[1], chunk, f, size[axes[0]] - 1, second, landing2)

    def last(chunk):
        for f, (axes, buffers, _) in enumerate(flows):
            for copy in flight[(chunk, f)]:
                copy.wait()
            _, _, second, landing2, (third, landing3) = buffers

            def one(i, carry, axis=axes[1], second=second, landing2=landing2, third=third):
                total = second[chunk, me[axis], i].astype(F32)
                for d in range(size[axis] - 1):
                    total = total + landing2[chunk, d, i].astype(F32)
                third[chunk, i] = total.astype(BF16)
                return carry

            lax.fori_loop(0, size["z"], one, 0)
            before = size["x"] + size["y"] - 2
            flight[(chunk, f)] = exchange("z", chunk, f, before, third, landing3)

    def finish(chunk):
        for f, (axes, buffers, offset) in enumerate(flows):
            for copy in flight[(chunk, f)]:
                copy.wait()
            third, landing3 = buffers[4]
            total = third[chunk, me["z"]].astype(F32)
            for d in range(size["z"] - 1):
                total = total + landing3[chunk, d].astype(F32)
            lo = chunk * width + offset
            out_ref[:, lo : lo + half] = total

    steps = (begin, middle, last, finish)
    for tick in range(chunks + len(steps) - 1):
        for number in reversed(range(len(steps))):
            if 0 <= tick - number < chunks:
                steps[number](tick - number)


def sum_experts(part, size, collective_id):
    chunks, rows, width = part.shape[0], part.shape[-2], part.shape[-1]
    half = width // 2
    x, y, z = size["x"], size["y"], size["z"]

    def buffer(*lead):
        return pltpu.VMEM((chunks,) + lead + (rows, half), BF16)

    def buffers(a, b):
        return [buffer(a, b, z), buffer(a - 1, b, z), buffer(b, z), buffer(b - 1, z), buffer(z), buffer(z - 1)]

    hops = 2 * chunks * (x + y + z - 3)

    def kernel(part_ref, out_ref, *scratch):
        a, b = list(scratch[4:10]), list(scratch[10:16])
        experts_kernel(
            size, part_ref, out_ref, *scratch[:4], *a[:4], tuple(a[4:]), *b[:4], tuple(b[4:])
        )

    return pl.pallas_call(
        kernel,
        out_shape=jax.ShapeDtypeStruct((rows, chunks * width), F32),
        in_specs=[pl.BlockSpec(memory_space=pltpu.VMEM)],
        out_specs=pl.BlockSpec(memory_space=pltpu.VMEM),
        scratch_shapes=[
            pltpu.VMEM((chunks, z, x, y, rows, width), BF16),
            pltpu.SemaphoreType.DMA((chunks,)),
            pltpu.SemaphoreType.DMA((chunks,)),
            pltpu.SemaphoreType.DMA((2, hops)),
        ]
        + buffers(y, x)
        + buffers(x, y),
        compiler_params=pltpu.CompilerParams(
            collective_id=collective_id, has_side_effects=True, vmem_limit_bytes=VMEM_BYTES
        ),
        name="sum_experts",
    )(part)


def hidden_kernel(rows_ref, gate_ref, up_ref, out_ref):
    rows = rows_ref[...]
    gate = jnp.dot(rows, gate_ref[0], preferred_element_type=F32)
    up = jnp.dot(rows, up_ref[0], preferred_element_type=F32)
    out_ref[...] = (gate * jax.nn.sigmoid(gate) * up).astype(BF16)


def down_kernel(hidden_ref, down_ref, share_ref, out_ref):
    part = jnp.dot(hidden_ref[...], down_ref[0], preferred_element_type=F32)
    out_ref[...] = (part * share_ref[...]).astype(BF16)


def feed_forward(rows, share, w_gate, w_up, w_down, chunks):
    count, features, units = rows.shape[0], w_gate.shape[1], w_gate.shape[2]
    tall = 512 if count % 512 == 0 else count
    tile = 256 if units % 256 == 0 else units
    weight = pl.BlockSpec((1, features, tile), lambda n, m: (0, 0, n))
    params = pltpu.CompilerParams(vmem_limit_bytes=VMEM_BYTES)
    hidden = pl.pallas_call(
        hidden_kernel,
        grid=(units // tile, count // tall),
        out_shape=jax.ShapeDtypeStruct((count, units), BF16),
        in_specs=[pl.BlockSpec((tall, features), lambda n, m: (m, 0)), weight, weight],
        out_specs=pl.BlockSpec((tall, tile), lambda n, m: (m, n)),
        compiler_params=params,
        name="hidden_units",
    )(rows, w_gate, w_up)
    width = features // chunks
    return pl.pallas_call(
        down_kernel,
        grid=(chunks, count // tall),
        out_shape=jax.ShapeDtypeStruct((chunks, count, width), BF16),
        in_specs=[
            pl.BlockSpec((tall, units), lambda n, m: (m, 0)),
            pl.BlockSpec((1, units, width), lambda n, m: (0, 0, n)),
            pl.BlockSpec((tall, 1), lambda n, m: (m, 0)),
        ],
        out_specs=pl.BlockSpec((None, tall, width), lambda n, m: (n, m, 0)),
        compiler_params=params,
        name="down",
    )(hidden, w_down, share)


def lane_tiles(column, lanes):
    return jnp.concatenate([column] * (lanes // column.shape[1]), axis=1)


def end_kernel(delta_ref, drive_ref, input_ref, rate_ref, end_ref):
    rate = -jnp.exp(rate_ref[...])
    lanes = rate.shape[1]

    def step(t, state):
        decay = jnp.exp(delta_ref[pl.ds(t, 1), :] * rate)
        return decay * state + drive_ref[pl.ds(t, 1), :] * lane_tiles(input_ref[t], lanes)

    end_ref[...] = lax.fori_loop(0, delta_ref.shape[0], step, jnp.zeros_like(rate), unroll=8)


def scan_kernel(
    delta_ref, drive_ref, input_ref, output_ref, rate_ref, start_ref, conv_ref, gate_ref, skip_ref, out_ref, y_ref
):
    rate = -jnp.exp(rate_ref[...])
    lanes = rate.shape[1]

    def step(t, state):
        decay = jnp.exp(delta_ref[pl.ds(t, 1), :] * rate)
        state = decay * state + drive_ref[pl.ds(t, 1), :] * lane_tiles(input_ref[t], lanes)
        y_ref[pl.ds(t, 1), :] = jnp.sum(state * lane_tiles(output_ref[t], lanes), axis=0, keepdims=True)
        return state

    lax.fori_loop(0, delta_ref.shape[0], step, start_ref[...], unroll=8)
    scan_out = y_ref[...] + skip_ref[...] * conv_ref[...].astype(F32)
    gate = gate_ref[...].astype(F32)
    out_ref[...] = (scan_out * (gate * jax.nn.sigmoid(gate))).astype(BF16)


def scan_specs(rows, states, lanes):
    wide = pl.BlockSpec((rows, lanes), lambda i: (0, i))
    maps = pl.BlockSpec((rows, states, 128), lambda i: (0, 0, 0))
    state = pl.BlockSpec((states, lanes), lambda i: (0, i))
    return wide, maps, state, pl.BlockSpec((1, lanes), lambda i: (0, i))


def body(
    mixer_input,
    gate_input,
    conv_weight,
    conv_bias,
    rank_weight,
    state_weight,
    delta_weight,
    delta_bias,
    log_rates,
    skip_gain,
    out_proj,
    residual,
    norm_gain,
    router,
    w_gate,
    w_up,
    w_down,
    routes,
):
    seq, exp = lax.axis_size("seq"), lax.axis_size("exp")
    size = axis_sizes(seq, exp)
    taps = conv_weight.shape[0]
    block_rows, width = mixer_input.shape
    route = [(i - 1, i) for i in range(1, seq)]
    rim_rows = lax.ppermute(mixer_input[block_rows - (taps - 1) :], "seq", route)
    padded = jnp.concatenate([rim_rows, mixer_input], axis=0)
    conv_sum = jnp.zeros(mixer_input.shape, F32) + conv_bias[None, :]
    for offset in range(taps):
        conv_sum = conv_sum + conv_weight[offset].astype(F32)[None, :] * padded[
            offset : offset + block_rows
        ].astype(F32)
    conv_act = jax.nn.silu(conv_sum).astype(BF16)
    rank, states = rank_weight.shape[1], log_rates.shape[0]
    narrow = -(-(rank + 2 * states) // 128) * 128
    low_weight = jnp.concatenate(
        [rank_weight, state_weight, jnp.zeros((width, narrow - rank - 2 * states), BF16)], axis=1
    )
    low_part = jnp.dot(conv_act, low_weight, preferred_element_type=F32)
    low = jnp.sum(gather(low_part, size, ("yc",), (), 1), axis=(0, 1))
    delta_low = low[:, :rank].astype(BF16)
    input_map = low[:, rank : rank + states]
    output_map = low[:, rank + states : rank + 2 * states]
    delta = jax.nn.softplus(
        jnp.dot(delta_low, delta_weight, preferred_element_type=F32) + delta_bias[None, :]
    )
    drive = delta * conv_act.astype(F32)
    total_dt = jnp.sum(delta, axis=0)
    input_wide = jnp.broadcast_to(input_map[:, :, None], (block_rows, states, 128))
    output_wide = jnp.broadcast_to(output_map[:, :, None], (block_rows, states, 128))

    lanes = 512 if width % 512 == 0 else 128
    wide, maps, state, line = scan_specs(block_rows, states, lanes)
    last = pl.pallas_call(
        end_kernel,
        grid=(width // lanes,),
        out_shape=jax.ShapeDtypeStruct((states, width), F32),
        in_specs=[wide, wide, maps, state],
        out_specs=state,
        name="block_end",
    )(delta, drive, input_wide, log_rates)
    passing = jnp.concatenate([last, total_dt.reshape(states, width // states)], axis=1).astype(BF16)
    passed = gather(passing, size, ("zx",) * 2, (width // 2,), 2).reshape((seq,) + passing.shape)
    index = lax.axis_index("seq")
    rate = jnp.exp(log_rates)
    start_state = jnp.zeros((states, width), F32)
    for k in range(seq - 1):
        gone = passed[k, :, width:].reshape(1, width).astype(F32)
        following = jnp.exp(-gone * rate) * start_state + passed[k, :, :width].astype(F32)
        start_state = jnp.where(k < index, following, start_state)
    gated = pl.pallas_call(
        scan_kernel,
        grid=(width // lanes,),
        out_shape=jax.ShapeDtypeStruct((block_rows, width), BF16),
        in_specs=[wide, wide, maps, maps, state, state, wide, wide, line],
        out_specs=wide,
        scratch_shapes=[pltpu.VMEM((block_rows, lanes), F32)],
        name="scan",
    )(delta, drive, input_wide, output_wide, log_rates, start_state, conv_act, gate_input, skip_gain[None, :])

    tok_dev, features = residual.shape
    everyone = gather(gated, size, ("zx",) * 4, tuple(k * width // 4 for k in range(1, 4)), 3).reshape(seq * block_rows, width)
    part = jnp.dot(everyone, out_proj, preferred_element_type=F32).astype(BF16)
    part = part.reshape(seq, exp, tok_dev, part.shape[1]).transpose(1, 0, 2, 3)
    hidden = residual.astype(F32) + sum_channels(part, size, 4)
    mean_square = jnp.mean(hidden * hidden, axis=1, keepdims=True)
    normed = (hidden * lax.rsqrt(mean_square + 1e-05) * norm_gain[None, :]).astype(BF16)
    logits = jnp.dot(normed.astype(F32), router, precision=lax.Precision.HIGHEST)
    experts = router.shape[1]
    expert_ids = jnp.arange(experts, dtype=jnp.int32)
    matches = (routes[:, :, None] == expert_ids[None, None, :]).astype(F32)
    chosen = jnp.sum(matches * logits[:, None, :], axis=2)
    route_weights = jax.nn.sigmoid(chosen - chosen[:, ::-1])
    shares = jnp.sum(matches * route_weights[:, :, None], axis=1)
    shares = jnp.pad(shares, ((0, 0), (0, 128 - experts))).astype(BF16)
    rows = gather(
        jnp.concatenate([normed, shares], axis=1), size, ("zxyc", "zyxc"), (features // 2,), 5
    )
    rows = rows.reshape(seq * exp * tok_dev, features + 128)
    own_share = jnp.sum(
        jnp.where(
            jnp.arange(128)[None, :] == lax.axis_index("exp"), rows[:, features:].astype(F32), 0.0
        ),
        axis=1,
        keepdims=True,
    )
    chunks = 4
    part = feed_forward(rows, own_share, w_gate, w_up, w_down, chunks)
    part = part.reshape(
        chunks, size["z"], size["x"], size["y"], size["c"], tok_dev, features // chunks
    )
    moe_sum = sum_experts(part, size, 6)
    return ((hidden + moe_sum).astype(BF16), moe_sum)


def solution(mesh):
    in_specs = (
        P("seq", "exp"),
        P("seq", "exp"),
        P(None, "exp"),
        P("exp"),
        P("exp", None),
        P("exp", None),
        P(None, "exp"),
        P("exp"),
        P(None, "exp"),
        P("exp"),
        P("exp", "seq"),
        P(("seq", "exp"), None),
        P(),
        P(),
        P("exp", None, "seq"),
        P("exp", None, "seq"),
        P("exp", "seq", None),
        P(("seq", "exp"), None),
    )
    out_specs = (P(("seq", "exp"), None), P(("seq", "exp"), None))
    return jax.shard_map(body, mesh=mesh, in_specs=in_specs, out_specs=out_specs, check_vma=False)
```

```python
import functools

import jax
import jax.numpy as jnp
from jax import lax
from jax.experimental import pallas as pl
from jax.experimental.pallas import tpu as pltpu
from jax.sharding import PartitionSpec as P

MESH = pl.DeviceIdType.MESH
BF16 = jnp.bfloat16
F32 = jnp.float32
VMEM_BYTES = 58 * 1024 * 1024
ORDER = "zxyc"


def axis_sizes(seq, exp):
    x = 1
    while 4 * x * x <= seq and seq % (2 * x) == 0:
        x *= 2
    c = 2 if exp % 2 == 0 else 1
    return {"z": seq // x, "x": x, "y": exp // c, "c": c}


def own_place(size):
    seq, exp = lax.axis_index("seq"), lax.axis_index("exp")
    return {"z": seq // size["x"], "x": seq % size["x"], "y": exp // size["c"], "c": exp % size["c"]}


def device_at(place, size):
    return (place["z"] * size["x"] + place["x"], place["y"] * size["c"] + place["c"])


def moved(place, size, axis, distance):
    return {**place, axis: (place[axis] + distance) % size[axis]}


def greet(size, axes):
    me = own_place(size)
    barrier = pltpu.get_barrier_semaphore()
    count = 0
    for axis in axes:
        for d in range(1, size[axis]):
            pl.semaphore_signal(
                barrier, inc=1, device_id=device_at(moved(me, size, axis, d), size), device_id_type=MESH
            )
            count += 1
    pl.semaphore_wait(barrier, count)


def held_after(size, axes):
    held = [()]
    for axis in axes:
        held = [h + (d,) for h in held for d in range(size[axis])]
    return held


def gather_kernel(size, flows, x_ref, out_ref, send_sem, recv_sem, own_sem):
    me = own_place(size)
    axes = [a for a in ORDER if a in flows[0][0]]
    greet(size, axes)

    def slot(offsets, path):
        place = dict(me)
        for axis, d in zip(path, offsets):
            place[axis] = (me[axis] + d) % size[axis]
        return tuple(place[a] for a in axes)

    own = pltpu.make_async_copy(x_ref, out_ref.at[slot((), ())], own_sem)
    own.start()
    sends, arrived, number = [], set(), {}
    for f, (path, _, _) in enumerate(flows):
        for offsets in held_after(size, path):
            number[(f, offsets)] = len(number)

    def window(ref, lo, hi):
        return ref.at[:, lo:hi]

    def arrive(f, offsets):
        path, lo, hi = flows[f]
        full = offsets + (0,) * (len(path) - len(offsets))
        if any(full) and (f, full) not in arrived:
            arrived.add((f, full))
            landing = window(out_ref.at[slot(full, path)], lo, hi)
            pltpu.make_async_copy(landing, landing, recv_sem.at[number[(f, full)]]).wait()

    def forward(f, offsets, stage):
        path, lo, hi = flows[f]
        here = slot(offsets, path)
        axis = path[stage]
        source = x_ref if not any(offsets) else out_ref.at[here]
        for d in range(1, size[axis]):
            lands = offsets[:stage] + (size[axis] - d,) + (0,) * (len(path) - stage - 1)
            copy = pltpu.make_async_remote_copy(
                src_ref=window(source, lo, hi),
                dst_ref=window(out_ref.at[here], lo, hi),
                send_sem=send_sem.at[len(sends)],
                recv_sem=recv_sem.at[number[(f, lands)]],
                device_id=device_at(moved(me, size, axis, d), size),
                device_id_type=MESH,
            )
            copy.start()
            sends.append(copy)

    stages = len(flows[0][0])
    for stage in range(stages):
        for f, (path, _, _) in enumerate(flows):
            forward(f, (0,) * stages, stage)
    alike = all(path == flows[0][0] for path, _, _ in flows)
    for came in range(stages):
        work = []
        for f, (path, _, _) in enumerate(flows):
            held = [h for h in held_after(size, path[: came + 1]) if h[came]]
            work += [(f if alike else k, f, h + (0,) * (stages - came - 1)) for k, h in enumerate(held)]
        for _, f, offsets in sorted(work, key=lambda item: item[0]):
            arrive(f, offsets)
            for stage in range(came + 1, stages):
                forward(f, offsets, stage)
    for f, (path, _, _) in enumerate(flows):
        for offsets in held_after(size, path):
            arrive(f, offsets)
    for copy in sends:
        copy.wait_send()
    own.wait()


def gather(block, size, paths, splits, collective_id):
    axes = [a for a in ORDER if a in paths[0]]
    edges = (0,) + tuple(splits) + (block.shape[1],)
    flows = [(tuple(p), lo, hi) for p, lo, hi in zip(paths, edges[:-1], edges[1:])]
    slots = len(flows)
    for a in axes:
        slots *= size[a]
    return pl.pallas_call(
        functools.partial(gather_kernel, size, flows),
        out_shape=jax.ShapeDtypeStruct(tuple(size[a] for a in axes) + block.shape, block.dtype),
        in_specs=[pl.BlockSpec(memory_space=pl.ANY)],
        out_specs=pl.BlockSpec(memory_space=pl.ANY),
        scratch_shapes=[
            pltpu.SemaphoreType.DMA((slots,)),
            pltpu.SemaphoreType.DMA((slots,)),
            pltpu.SemaphoreType.DMA,
        ],
        compiler_params=pltpu.CompilerParams(
            collective_id=collective_id, has_side_effects=True, vmem_limit_bytes=VMEM_BYTES
        ),
        name="gather_" + "".join(axes),
    )(block)


def channels_kernel(size, part_ref, out_ref, landed, summed, spread, send_sem, recv_sem, send2, recv2):
    seq, exp = size["z"] * size["x"], size["y"] * size["c"]
    s, e = lax.axis_index("seq"), lax.axis_index("exp")
    barrier = pltpu.get_barrier_semaphore()
    for d in range(1, exp):
        pl.semaphore_signal(barrier, inc=1, device_id=(s, (e + d) % exp), device_id_type=MESH)
    for d in range(1, seq):
        pl.semaphore_signal(barrier, inc=1, device_id=((s + d) % seq, e), device_id_type=MESH)
    pl.semaphore_wait(barrier, exp + seq - 2)
    copies = []
    for d in range(1, exp):
        to = (e + d) % exp
        copy = pltpu.make_async_remote_copy(
            src_ref=part_ref.at[to],
            dst_ref=landed.at[exp - d - 1],
            send_sem=send_sem.at[d - 1],
            recv_sem=recv_sem.at[exp - d - 1],
            device_id=(s, to),
            device_id_type=MESH,
        )
        copy.start()
        copies.append(copy)
    for copy in copies:
        copy.wait()

    def add(k, carry):
        total = part_ref[e, k].astype(F32)
        for d in range(exp - 1):
            total = total + landed[d, k].astype(F32)
        summed[k] = total.astype(BF16)
        return carry

    lax.fori_loop(0, seq, add, 0)
    copies = []
    for d in range(1, seq):
        to = (s + d) % seq
        copy = pltpu.make_async_remote_copy(
            src_ref=summed.at[to],
            dst_ref=spread.at[s],
            send_sem=send2.at[d - 1],
            recv_sem=recv2.at[seq - d - 1],
            device_id=(to, e),
            device_id_type=MESH,
        )
        copy.start()
        copies.append(copy)
    for copy in copies:
        copy.wait_send()
    for d in range(1, seq):
        block = spread.at[(s + d) % seq]
        pltpu.make_async_copy(block, block, recv2.at[d - 1]).wait()
    spread[s] = summed[s]
    width = spread.shape[2]
    for k in range(seq):
        out_ref[:, k * width : (k + 1) * width] = spread[k].astype(F32)


def sum_channels(part, size, collective_id):
    exp, seq, rows, width = part.shape
    return pl.pallas_call(
        functools.partial(channels_kernel, size),
        out_shape=jax.ShapeDtypeStruct((rows, seq * width), F32),
        in_specs=[pl.BlockSpec(memory_space=pltpu.VMEM)],
        out_specs=pl.BlockSpec(memory_space=pltpu.VMEM),
        scratch_shapes=[
            pltpu.VMEM((exp - 1, seq, rows, width), BF16),
            pltpu.VMEM((seq, rows, width), BF16),
            pltpu.VMEM((seq, rows, width), BF16),
            pltpu.SemaphoreType.DMA((exp - 1,)),
            pltpu.SemaphoreType.DMA((exp - 1,)),
            pltpu.SemaphoreType.DMA((seq - 1,)),
            pltpu.SemaphoreType.DMA((seq - 1,)),
        ],
        compiler_params=pltpu.CompilerParams(
            collective_id=collective_id, has_side_effects=True, vmem_limit_bytes=VMEM_BYTES
        ),
        name="sum_channels",
    )(part)


def experts_kernel(size, hidden_ref, share_ref, down_ref, out_ref, weight, weight_sem, part_ref, *scratch):
    me = own_place(size)
    fetches = []
    for chunk in range(part_ref.shape[0]):
        wide = part_ref.shape[-1]
        fetch = pltpu.make_async_copy(
            down_ref.at[0, :, chunk * wide : (chunk + 1) * wide], weight.at[chunk], weight_sem.at[chunk]
        )
        fetch.start()
        fetches.append(fetch)
    greet(size, "zxyc")
    chunks = part_ref.shape[0]
    width = part_ref.shape[-1]
    half = width // 2
    from_core, core_send, core_recv, sems = scratch[:4]
    flows = (("yxz", scratch[4:9], 0), ("xyz", scratch[9:14], half))
    hops = sum(size[a] - 1 for a in "xyz")

    def exchange(axis, chunk, flow, before, source, landing):
        copies = []
        base = (chunk * 2 + flow) * hops + before
        for d in range(1, size[axis]):
            to = moved(me, size, axis, d)
            copy = pltpu.make_async_remote_copy(
                src_ref=source.at[chunk, to[axis]],
                dst_ref=landing.at[chunk, size[axis] - d - 1],
                send_sem=sems.at[0, base + d - 1],
                recv_sem=sems.at[1, base + size[axis] - d - 1],
                device_id=device_at(to, size),
                device_id_type=MESH,
            )
            copy.start()
            copies.append(copy)
        return copies

    core_copies = []
    lead = part_ref.shape[2:-1]
    per_plane = 1
    for extent in lead:
        per_plane *= extent

    def multiply(chunk):
        fetches[chunk].wait()

        def plane(k, carry):
            rows = pl.ds(k * per_plane, per_plane)
            product = jnp.dot(hidden_ref[rows, :], weight[chunk], preferred_element_type=F32)
            product = (product * share_ref[rows, :]).astype(BF16)
            part_ref[chunk, k] = product.reshape(lead + (width,))
            return carry

        def whole():
            product = jnp.dot(hidden_ref[...], weight[chunk], preferred_element_type=F32)
            product = (product * share_ref[...]).astype(BF16)
            part_ref[chunk] = product.reshape((size["z"],) + lead + (width,))

        if hidden_ref.shape[0] <= 512:
            whole()
        else:
            lax.fori_loop(0, size["z"], plane, 0)
        if size["c"] == 2:
            copy = pltpu.make_async_remote_copy(
                src_ref=part_ref.at[chunk, :, :, :, 1 - me["c"]],
                dst_ref=from_core.at[chunk],
                send_sem=core_send.at[chunk],
                recv_sem=core_recv.at[chunk],
                device_id=device_at(moved(me, size, "c", 1), size),
                device_id_type=MESH,
            )
            copy.start()
            core_copies.append(copy)
    flight = {}

    def begin(chunk):
        if core_copies:
            core_copies[chunk].wait()

        def first(i, carry):
            z, x, y = i // (size["x"] * size["y"]), (i // size["y"]) % size["x"], i % size["y"]
            total = part_ref[chunk, z, x, y, me["c"]].astype(F32)
            if core_copies:
                total = total + from_core[chunk, z, x, y].astype(F32)
            total = total.astype(BF16)
            flows[0][1][0][chunk, y, x, z] = total[:, :half]
            flows[1][1][0][chunk, x, y, z] = total[:, half:]
            return carry

        lax.fori_loop(0, size["x"] * size["y"] * size["z"], first, 0)
        for f, (axes, buffers, _) in enumerate(flows):
            flight[(chunk, f)] = exchange(axes[0], chunk, f, 0, buffers[0], buffers[1])

    def middle(chunk):
        for f, (axes, buffers, _) in enumerate(flows):
            for copy in flight[(chunk, f)]:
                copy.wait()
            source, landing, second, landing2, _ = buffers
            inner = size["z"]

            def one(i, carry, axis=axes[0], source=source, landing=landing, second=second):
                total = source[chunk, me[axis], i // inner, i % inner].astype(F32)
                for d in range(size[axis] - 1):
                    total = total + landing[chunk, d, i // inner, i % inner].astype(F32)
                second[chunk, i // inner, i % inner] = total.astype(BF16)
                return carry

            lax.fori_loop(0, size[axes[1]] * inner, one, 0)
            flight[(chunk, f)] = exchange(axes[1], chunk, f, size[axes[0]] - 1, second, landing2)

    def last(chunk):
        for f, (axes, buffers, _) in enumerate(flows):
            for copy in flight[(chunk, f)]:
                copy.wait()
            _, _, second, landing2, (third, landing3) = buffers

            def one(i, carry, axis=axes[1], second=second, landing2=landing2, third=third):
                total = second[chunk, me[axis], i].astype(F32)
                for d in range(size[axis] - 1):
                    total = total + landing2[chunk, d, i].astype(F32)
                third[chunk, i] = total.astype(BF16)
                return carry

            lax.fori_loop(0, size["z"], one, 0)
            before = size["x"] + size["y"] - 2
            flight[(chunk, f)] = exchange("z", chunk, f, before, third, landing3)

    def finish(chunk):
        for f, (axes, buffers, offset) in enumerate(flows):
            for copy in flight[(chunk, f)]:
                copy.wait()
            third, landing3 = buffers[4]
            total = third[chunk, me["z"]].astype(F32)
            for d in range(size["z"] - 1):
                total = total + landing3[chunk, d].astype(F32)
            lo = chunk * width + offset
            out_ref[:, lo : lo + half] = total

    steps = (multiply, begin, middle, last, finish)
    for tick in range(chunks + len(steps) - 1):
        for number in (0, 4, 3, 2, 1):
            if 0 <= tick - number < chunks:
                steps[number](tick - number)


def sum_experts(hidden, share, w_down, size, rows, chunks, collective_id):
    units, features = w_down.shape[1:]
    width = features // chunks
    half = width // 2
    x, y, z = size["x"], size["y"], size["z"]

    def buffer(*lead):
        return pltpu.VMEM((chunks,) + lead + (rows, half), BF16)

    def buffers(a, b):
        return [buffer(a, b, z), buffer(a - 1, b, z), buffer(b, z), buffer(b - 1, z), buffer(z), buffer(z - 1)]

    hops = 2 * chunks * (x + y + z - 3)

    def kernel(hidden_ref, share_ref, down_ref, out_ref, weight, weight_sem, part_ref, *scratch):
        a, b = list(scratch[4:10]), list(scratch[10:16])
        experts_kernel(
            size, hidden_ref, share_ref, down_ref, out_ref, weight, weight_sem, part_ref,
            *scratch[:4], *a[:4], tuple(a[4:]), *b[:4], tuple(b[4:])
        )

    return pl.pallas_call(
        kernel,
        out_shape=jax.ShapeDtypeStruct((rows, chunks * width), F32),
        in_specs=[
            pl.BlockSpec(memory_space=pltpu.VMEM),
            pl.BlockSpec(memory_space=pltpu.VMEM),
            pl.BlockSpec(memory_space=pl.ANY),
        ],
        out_specs=pl.BlockSpec(memory_space=pltpu.VMEM),
        scratch_shapes=[
            pltpu.VMEM((chunks, units, width), BF16),
            pltpu.SemaphoreType.DMA((chunks,)),
            pltpu.VMEM((chunks, z, x, y, size["c"], rows, width), BF16),
            pltpu.VMEM((chunks, z, x, y, rows, width), BF16),
            pltpu.SemaphoreType.DMA((chunks,)),
            pltpu.SemaphoreType.DMA((chunks,)),
            pltpu.SemaphoreType.DMA((2, hops)),
        ]
        + buffers(y, x)
        + buffers(x, y),
        compiler_params=pltpu.CompilerParams(
            collective_id=collective_id, has_side_effects=True, vmem_limit_bytes=VMEM_BYTES
        ),
        name="sum_experts",
    )(hidden, share, w_down)


def hidden_kernel(rows_ref, gate_ref, up_ref, out_ref):
    rows = rows_ref[...]
    gate = jnp.dot(rows, gate_ref[0], preferred_element_type=F32)
    up = jnp.dot(rows, up_ref[0], preferred_element_type=F32)
    out_ref[...] = (gate * jax.nn.sigmoid(gate) * up).astype(BF16)


def hidden_units(rows, w_gate, w_up):
    count, features, units = rows.shape[0], w_gate.shape[1], w_gate.shape[2]
    tall = 512 if count % 512 == 0 else count
    tile = 256 if units % 256 == 0 else units
    weight = pl.BlockSpec((1, features, tile), lambda n, m: (0, 0, n))
    params = pltpu.CompilerParams(vmem_limit_bytes=VMEM_BYTES)
    return pl.pallas_call(
        hidden_kernel,
        grid=(units // tile, count // tall),
        out_shape=jax.ShapeDtypeStruct((count, units), BF16),
        in_specs=[pl.BlockSpec((tall, features), lambda n, m: (m, 0)), weight, weight],
        out_specs=pl.BlockSpec((tall, tile), lambda n, m: (m, n)),
        compiler_params=params,
        name="hidden_units",
    )(rows, w_gate, w_up)


def lane_tiles(column, lanes):
    return jnp.concatenate([column] * (lanes // column.shape[1]), axis=1)


def end_kernel(delta_ref, drive_ref, input_ref, rate_ref, end_ref):
    rate = -jnp.exp(rate_ref[...])
    lanes = rate.shape[1]

    def step(t, state):
        decay = jnp.exp(delta_ref[pl.ds(t, 1), :] * rate)
        return decay * state + drive_ref[pl.ds(t, 1), :] * lane_tiles(input_ref[t], lanes)

    end_ref[...] = lax.fori_loop(0, delta_ref.shape[0], step, jnp.zeros_like(rate), unroll=8)


def scan_kernel(
    delta_ref, drive_ref, input_ref, output_ref, rate_ref, start_ref, conv_ref, gate_ref, skip_ref, out_ref, y_ref
):
    rate = -jnp.exp(rate_ref[...])
    lanes = rate.shape[1]

    def step(t, state):
        decay = jnp.exp(delta_ref[pl.ds(t, 1), :] * rate)
        state = decay * state + drive_ref[pl.ds(t, 1), :] * lane_tiles(input_ref[t], lanes)
        y_ref[pl.ds(t, 1), :] = jnp.sum(state * lane_tiles(output_ref[t], lanes), axis=0, keepdims=True)
        return state

    lax.fori_loop(0, delta_ref.shape[0], step, start_ref[...], unroll=8)
    scan_out = y_ref[...] + skip_ref[...] * conv_ref[...].astype(F32)
    gate = gate_ref[...].astype(F32)
    out_ref[...] = (scan_out * (gate * jax.nn.sigmoid(gate))).astype(BF16)


def scan_specs(rows, states, lanes):
    wide = pl.BlockSpec((rows, lanes), lambda i: (0, i))
    maps = pl.BlockSpec((rows, states, 128), lambda i: (0, 0, 0))
    state = pl.BlockSpec((states, lanes), lambda i: (0, i))
    return wide, maps, state, pl.BlockSpec((1, lanes), lambda i: (0, i))


def body(
    mixer_input,
    gate_input,
    conv_weight,
    conv_bias,
    rank_weight,
    state_weight,
    delta_weight,
    delta_bias,
    log_rates,
    skip_gain,
    out_proj,
    residual,
    norm_gain,
    router,
    w_gate,
    w_up,
    w_down,
    routes,
):
    seq, exp = lax.axis_size("seq"), lax.axis_size("exp")
    size = axis_sizes(seq, exp)
    taps = conv_weight.shape[0]
    block_rows, width = mixer_input.shape
    route = [(i - 1, i) for i in range(1, seq)]
    rim_rows = lax.ppermute(mixer_input[block_rows - (taps - 1) :], "seq", route)
    padded = jnp.concatenate([rim_rows, mixer_input], axis=0)
    conv_sum = jnp.zeros(mixer_input.shape, F32) + conv_bias[None, :]
    for offset in range(taps):
        conv_sum = conv_sum + conv_weight[offset].astype(F32)[None, :] * padded[
            offset : offset + block_rows
        ].astype(F32)
    conv_act = jax.nn.silu(conv_sum).astype(BF16)
    rank, states = rank_weight.shape[1], log_rates.shape[0]
    narrow = -(-(rank + 2 * states) // 128) * 128
    low_weight = jnp.concatenate(
        [rank_weight, state_weight, jnp.zeros((width, narrow - rank - 2 * states), BF16)], axis=1
    )
    low_part = jnp.dot(conv_act, low_weight, preferred_element_type=F32)
    low = jnp.sum(gather(low_part, size, ("yc",), (), 1), axis=(0, 1))
    delta_low = low[:, :rank].astype(BF16)
    input_map = low[:, rank : rank + states]
    output_map = low[:, rank + states : rank + 2 * states]
    delta = jax.nn.softplus(
        jnp.dot(delta_low, delta_weight, preferred_element_type=F32) + delta_bias[None, :]
    )
    drive = delta * conv_act.astype(F32)
    total_dt = jnp.sum(delta, axis=0)
    input_wide = jnp.broadcast_to(input_map[:, :, None], (block_rows, states, 128))
    output_wide = jnp.broadcast_to(output_map[:, :, None], (block_rows, states, 128))

    lanes = 512 if width % 512 == 0 else 128
    wide, maps, state, line = scan_specs(block_rows, states, lanes)
    last = pl.pallas_call(
        end_kernel,
        grid=(width // lanes,),
        out_shape=jax.ShapeDtypeStruct((states, width), F32),
        in_specs=[wide, wide, maps, state],
        out_specs=state,
        name="block_end",
    )(delta, drive, input_wide, log_rates)
    passing = jnp.concatenate([last, total_dt.reshape(states, width // states)], axis=1).astype(BF16)
    passed = gather(passing, size, ("zx",) * 2, (width // 2,), 2).reshape((seq,) + passing.shape)
    index = lax.axis_index("seq")
    rate = jnp.exp(log_rates)
    start_state = jnp.zeros((states, width), F32)
    for k in range(seq - 1):
        gone = passed[k, :, width:].reshape(1, width).astype(F32)
        following = jnp.exp(-gone * rate) * start_state + passed[k, :, :width].astype(F32)
        start_state = jnp.where(k < index, following, start_state)
    gated = pl.pallas_call(
        scan_kernel,
        grid=(width // lanes,),
        out_shape=jax.ShapeDtypeStruct((block_rows, width), BF16),
        in_specs=[wide, wide, maps, maps, state, state, wide, wide, line],
        out_specs=wide,
        scratch_shapes=[pltpu.VMEM((block_rows, lanes), F32)],
        name="scan",
    )(delta, drive, input_wide, output_wide, log_rates, start_state, conv_act, gate_input, skip_gain[None, :])

    tok_dev, features = residual.shape
    everyone = gather(gated, size, ("zx",) * 4, tuple(k * width // 4 for k in range(1, 4)), 3).reshape(seq * block_rows, width)
    part = jnp.dot(everyone, out_proj, preferred_element_type=F32).astype(BF16)
    part = part.reshape(seq, exp, tok_dev, part.shape[1]).transpose(1, 0, 2, 3)
    hidden = residual.astype(F32) + sum_channels(part, size, 4)
    mean_square = jnp.mean(hidden * hidden, axis=1, keepdims=True)
    normed = (hidden * lax.rsqrt(mean_square + 1e-05) * norm_gain[None, :]).astype(BF16)
    logits = jnp.dot(normed.astype(F32), router, precision=lax.Precision.HIGHEST)
    experts = router.shape[1]
    expert_ids = jnp.arange(experts, dtype=jnp.int32)
    matches = (routes[:, :, None] == expert_ids[None, None, :]).astype(F32)
    chosen = jnp.sum(matches * logits[:, None, :], axis=2)
    route_weights = jax.nn.sigmoid(chosen - chosen[:, ::-1])
    shares = jnp.sum(matches * route_weights[:, :, None], axis=1)
    shares = jnp.pad(shares, ((0, 0), (0, 128 - experts))).astype(BF16)
    rows = gather(
        jnp.concatenate([normed, shares], axis=1), size, ("zxyc", "zyxc"), (features // 2,), 5
    )
    rows = rows.reshape(seq * exp * tok_dev, features + 128)
    own_share = jnp.sum(
        jnp.where(
            jnp.arange(128)[None, :] == lax.axis_index("exp"), rows[:, features:].astype(F32), 0.0
        ),
        axis=1,
        keepdims=True,
    )
    activated = hidden_units(rows, w_gate, w_up)
    moe_sum = sum_experts(activated, own_share, w_down, size, tok_dev, 4, 6)
    return ((hidden + moe_sum).astype(BF16), moe_sum)


def solution(mesh):
    in_specs = (
        P("seq", "exp"),
        P("seq", "exp"),
        P(None, "exp"),
        P("exp"),
        P("exp", None),
        P("exp", None),
        P(None, "exp"),
        P("exp"),
        P(None, "exp"),
        P("exp"),
        P("exp", "seq"),
        P(("seq", "exp"), None),
        P(),
        P(),
        P("exp", None, "seq"),
        P("exp", None, "seq"),
        P("exp", "seq", None),
        P(("seq", "exp"), None),
    )
    out_specs = (P(("seq", "exp"), None), P(("seq", "exp"), None))
    return jax.shard_map(body, mesh=mesh, in_specs=in_specs, out_specs=out_specs, check_vma=False)
```
